32 devices in a mesh: grp: 1, feat: 32 (over z, y, x, core), dp: 1.
Axes of the slice: x: 2, y: 2, z: 4, core: 2. Of those that a mesh axis runs over, the one named last changes fastest.
Arguments:
- archive: bfloat16 [1024, 65536], P('grp', 'feat'), may hold values from -6 to 6
- picks: int32 [512], P(('grp', 'dp')), may hold values from 0 to 1023
- first_factor: bfloat16 [256, 256, 256], P(('grp', 'feat')), may hold values from -0.375 to 0.375
- second_factor: bfloat16 [256, 256, 256], P(('grp', 'feat')), may hold values from -0.375 to 0.375
- targets: bfloat16 [512, 65536], P(('grp', 'dp'), 'feat'), may hold values from -6 to 6
Outputs:
- first_grad: float32 [256, 256, 256], P(('grp', 'feat'), 'dp')
- second_grad: float32 [256, 256, 256], P(('grp', 'feat'), 'dp')
The draws below stay inside these ranges and needn't reach their ends.
All inputs are finite; a program needn't handle non-finite values.
Results may differ from the reference program's by a relative error of at most 0.0095.
Values may be sent and summed in bfloat16 or wider, within the bound.
A program may use at most 64 MiB of HBM per device.

```python
import math
import jax
import jax.numpy as jnp
from jax import lax

BLK = 256
S_DEV = 512
ARCHIVE = 1024
FEATURES = 65536
BATCH = 512


def place_ends(values, rng, least, largest):
    longest = values.shape.index(max(values.shape))
    spots = []
    for shift in (0, 1):
        where = [jax.random.randint(jax.random.fold_in(rng, axis), (), 0, length) for axis, length in enumerate(values.shape)]
        where[longest] = (where[longest] + shift) % values.shape[longest]
        spots.append(tuple(where))
    return values.at[spots[0]].set(least).at[spots[1]].set(largest)


def block_levels(key, dims, cuts, smallest, largest):
    def one(dim, blocks):
        heights = jax.random.uniform(jax.random.fold_in(jax.random.fold_in(key, 6), dim), (blocks,), jnp.float32, smallest / len(cuts), largest / len(cuts))
        return jnp.repeat(jnp.exp(heights), dims[dim] // blocks).reshape((-1,) + (1,) * (len(dims) - dim - 1))

    gain = one(*cuts[0])
    for cut in cuts[1:]:
        gain = gain * one(*cut)
    return gain


def normal_values(rng, dims, scale, reach, shards=(), kind=jnp.bfloat16):
    result = jax.random.normal(rng, dims, jnp.float32) * scale
    if len(shards) > 0:
        result = block_levels(rng, dims, shards, -0.22, 0.18) * result
    return jnp.clip(result, min=-reach, max=reach).astype(kind)


def setup_inputs(seed: int = 0, part: int = 0) -> dict:
    key_of = jax.random.split(jax.random.key(seed), 6)
    own_keys = jax.random.split(jax.random.fold_in(key_of[5], part), 6)
    archive = normal_values(own_keys[0], (ARCHIVE, FEATURES), 1.0, 6.0, ((1, 32),))
    picks = place_ends(jax.random.randint(own_keys[1], (BATCH,), 0, ARCHIVE), jax.random.fold_in(own_keys[1], 1), 0, ARCHIVE - 1).astype(jnp.int32)
    first_factor = normal_values(own_keys[2], (BLK, BLK, BLK), BLK ** -0.5, 0.375, ((0, 32),))
    second_factor = normal_values(own_keys[3], (BLK, BLK, BLK), BLK ** -0.5, 0.375, ((0, 32),))
    targets = normal_values(own_keys[4], (BATCH, FEATURES), 1.0, 6.0, ((1, 32),))
    return dict(archive=archive, picks=picks, first_factor=first_factor, second_factor=second_factor, targets=targets)


def reference(archive, picks, first_factor, second_factor, targets):
    scale = 1.0 / math.sqrt(BATCH)
    rows = S_DEV
    count = BATCH // rows
    pick_blocks = picks.reshape(count, rows)
    target_blocks = targets.reshape(count, rows, BLK, BLK)
    w_first = first_factor.astype(jnp.float32)
    w_second = second_factor.astype(jnp.float32)

    def step(carry, item):
        grad_one, grad_two = carry
        index_rows, goal = item
        x = jnp.take(archive, index_rows, axis=0).reshape(rows, BLK, BLK).astype(jnp.float32)
        y_first = jnp.einsum('sia,iab->sib', x, w_first).astype(jnp.bfloat16)
        z = jnp.swapaxes(y_first, 1, 2)
        z_float = z.astype(jnp.float32)
        hidden = jax.nn.gelu(z_float).astype(jnp.bfloat16)
        hidden_f = hidden.astype(jnp.float32)
        pred = jnp.einsum('sji,jik->sjk', hidden_f, w_second)
        resid = ((pred - goal.astype(jnp.float32)) * scale).astype(jnp.bfloat16)
        resid_f = resid.astype(jnp.float32)
        grad_two = grad_two + jnp.einsum('sji,sjk->jik', hidden_f, resid_f)
        d_hidden = jnp.einsum('sjk,jik->sji', resid_f, w_second)
        d_z = jax.vjp(jax.nn.gelu, z_float)[1](d_hidden)[0].astype(jnp.bfloat16)
        d_first = jnp.swapaxes(d_z, 1, 2).astype(jnp.float32)
        grad_one = grad_one + jnp.einsum('sia,sib->iab', x, d_first)
        return ((grad_one, grad_two), None)
    start = jnp.zeros((BLK, BLK, BLK), jnp.float32)
    (grad_one, grad_two), unused = lax.scan(step, (start, start), (pick_blocks, target_blocks))
    return (grad_one, grad_two)
```

```python
import functools
import math

import jax
import jax.numpy as jnp
from jax import lax
from jax.experimental import pallas as pl
from jax.experimental.pallas import tpu as pltpu
from jax.sharding import PartitionSpec as P

BF16 = jnp.bfloat16
F32 = jnp.float32
CH = 128
ROOT = math.sqrt(2.0 / math.pi)
CUBE = 0.044715


def dot(a, b, ca, cb):
    return lax.dot_general(a, b, (((ca,), (cb,)), ((), ())), preferred_element_type=F32)


def flip(me, k, n):
    out = 0
    bit = 1
    while bit < n:
        out = out + ((me // bit + k // bit) % 2) * bit
        bit *= 2
    return out


def kernel(n, lb, scale, picks, arch_hbm, f1_hbm, f2_hbm, goal_hbm, g1_hbm, g2_hbm,
           arch, f1, f2, goal, f1t, xc, xt, send, recv, bsend, brecv, zbuf, dzbuf, g1, g2,
           in_sem, out_sem, send_sem, recv_sem, bsend_sem, brecv_sem):
    me = lax.axis_index("feat")
    width = n * lb
    rows = goal.shape[0]
    chunks = rows // CH
    patterns = arch.shape[0]
    cell = lb * lb
    per = width // cell
    groups = n // per
    part = per * lb

    loads = [
        pltpu.make_async_copy(src, dst, in_sem.at[t])
        for t, (src, dst) in enumerate(((f1_hbm, f1), (arch_hbm, arch), (f2_hbm, f2), (goal_hbm, goal)))
    ]
    for load in loads:
        load.start()

    barrier = pltpu.get_barrier_semaphore()

    def greet(k, carry):
        pl.semaphore_signal(barrier, inc=1, device_id={"feat": flip(me, k, n)}, device_id_type=pl.DeviceIdType.MESH)
        return carry

    lax.fori_loop(1, n, greet, 0)

    left = lax.broadcasted_iota(jnp.int32, (width, width), 0)
    right = lax.broadcasted_iota(jnp.int32, (width, width), 1)
    perm = ((right % lb) * part + right // lb == left).astype(BF16)

    loads[0].wait()

    def turn(i, carry):
        f1t[i] = f1[i].T
        return carry

    lax.fori_loop(0, lb, turn, 0)
    loads[1].wait()

    def copy_to(sbuf, rbuf, ssem, rsem, c, peer):
        return pltpu.make_async_remote_copy(
            src_ref=sbuf.at[c, peer], dst_ref=rbuf.at[c, me], send_sem=ssem.at[c], recv_sem=rsem.at[c],
            device_id={"feat": peer}, device_id_type=pl.DeviceIdType.MESH)

    def send_all(sbuf, rbuf, ssem, rsem, c):
        def one(t, carry):
            copy_to(sbuf, rbuf, ssem, rsem, c, flip(me, n - 1 - t, n)).start()
            return carry

        lax.fori_loop(0, n - 1, one, 0)
        rbuf[c, me] = sbuf[c, me]

    def await_all(buf, sem, c):
        block = buf.at[c, pl.ds(0, n - 1)]
        pltpu.make_async_copy(block, block, sem.at[c]).wait()

    for c in range(chunks):
        col = jnp.broadcast_to(picks[pl.ds(c, 1), :].astype(F32), (CH, CH)).T.astype(jnp.int32)
        col = jnp.concatenate([col] * (patterns // CH), axis=1)
        pick = (col == lax.broadcasted_iota(jnp.int32, (CH, patterns), 1)).astype(BF16)

        def forward(p, carry):
            both = []
            for h in range(2):
                i = p * 2 + h
                cols = pl.ds(pl.multiple_of(i * width, width), width)
                x = dot(pick, arch[:, cols], 1, 0).astype(BF16)
                xc[i] = x
                y = dot(f1t[i], x, 1, 1)
                both.append(y.reshape(n, lb, CH))
            at = pl.ds(pl.multiple_of(p * 2 * lb, 2 * lb), 2 * lb)
            send[c, :, at, :] = jnp.concatenate(both, axis=1).astype(BF16)
            return carry

        lax.fori_loop(0, lb // 2, forward, 0)
        if c == 0:
            pl.semaphore_wait(barrier, n - 1)
        send_all(send, recv, send_sem, recv_sem, c)

        def turn_x(i, carry):
            xt[c, i] = xc[i].T
            return carry

        lax.fori_loop(0, lb, turn_x, 0)

    loads[2].wait()
    loads[3].wait()

    for c in range(chunks):
        await_all(recv, recv_sem, c)

        def permute(g, carry):
            four = recv[c, pl.ds(g * per, per)].reshape(width, CH)
            z = dot(perm, four, 1, 0).reshape(lb, part, CH)
            zbuf[:, pl.ds(pl.multiple_of(g * part, part), part), :] = z
            return carry

        lax.fori_loop(0, groups, permute, 0)

        def middle(j, carry):
            z = zbuf[j]
            sq = z * z
            t = jnp.tanh(ROOT * z * (1.0 + CUBE * sq))
            half = 0.5 * (1.0 + t)
            hidden = (z * half).astype(BF16)
            slope = half + 0.5 * z * (1.0 - t * t) * (ROOT * (1.0 + 3.0 * CUBE * sq))
            pred = dot(hidden, f2[j], 0, 0)
            cols = pl.ds(pl.multiple_of(j * width, width), width)
            want = goal[c * CH:(c + 1) * CH, cols].astype(F32)
            resid = ((pred - want) * scale).astype(BF16)
            grad = dot(hidden, resid, 1, 0)
            if c == 0:
                g2[j] = grad
            else:
                g2[j] += grad
            dh = dot(f2[j], resid, 1, 1)
            dzbuf[j] = (dh * slope).astype(BF16)
            return carry

        lax.fori_loop(0, lb, middle, 0)

        def back(g, carry):
            rows_in = dzbuf[:, pl.ds(pl.multiple_of(g * part, part), part), :].reshape(width, CH)
            out = dot(perm, rows_in, 0, 0).astype(BF16)
            bsend[c, pl.ds(g * per, per)] = out.reshape(per, cell, CH)
            return carry

        lax.fori_loop(0, groups, back, 0)
        send_all(bsend, brecv, bsend_sem, brecv_sem, c)

    out2 = pltpu.make_async_copy(g2, g2_hbm, out_sem.at[0])
    out2.start()

    for c in range(chunks):
        await_all(brecv, brecv_sem, c)

        def last(p, carry):
            at = pl.ds(pl.multiple_of(p * 2 * lb, 2 * lb), 2 * lb)
            both = brecv[c, :, at, :].astype(F32)
            for h in range(2):
                i = p * 2 + h
                d = both[:, h * lb:(h + 1) * lb, :].reshape(width, CH).astype(BF16)
                grad = dot(xt[c, i], d, 1, 1)
                if c == 0:
                    g1[i] = grad
                else:
                    g1[i] += grad
            return carry

        lax.fori_loop(0, lb // 2, last, 0)

    out1 = pltpu.make_async_copy(g1, g1_hbm, out_sem.at[1])
    out1.start()
    for c in range(chunks):
        await_all(send, send_sem, c)
        await_all(bsend, bsend_sem, c)
    out2.wait()
    out1.wait()


def fused(n, archive, picks, first_factor, second_factor, targets, scale):
    rows = picks.shape[0]
    lb, width, _ = first_factor.shape
    chunks = rows // CH
    any_ = pl.BlockSpec(memory_space=pl.ANY)
    grads = jax.ShapeDtypeStruct((lb, width, width), F32)
    block = pltpu.VMEM((chunks, n, lb * lb, CH), BF16)
    dma = pltpu.SemaphoreType.DMA
    return pl.pallas_call(
        functools.partial(kernel, n, lb, scale),
        out_shape=(grads, grads),
        in_specs=[pl.BlockSpec(memory_space=pltpu.VMEM)] + [any_] * 4,
        out_specs=(any_, any_),
        scratch_shapes=[
            pltpu.VMEM(archive.shape, BF16),
            pltpu.VMEM(first_factor.shape, BF16),
            pltpu.VMEM(second_factor.shape, BF16),
            pltpu.VMEM(targets.shape, BF16),
            pltpu.VMEM(first_factor.shape, BF16),
            pltpu.VMEM((lb, CH, width), BF16),
            pltpu.VMEM((chunks, lb, width, CH), BF16),
            block, block, block, block,
            pltpu.VMEM((lb, width, CH), F32),
            pltpu.VMEM((lb, width, CH), BF16),
            pltpu.VMEM((lb, width, width), F32),
            pltpu.VMEM((lb, width, width), F32),
            dma((4,)), dma((2,)),
            dma((chunks,)), dma((chunks,)), dma((chunks,)), dma((chunks,)),
        ],
        compiler_params=pltpu.CompilerParams(
            collective_id=0, has_side_effects=True, vmem_limit_bytes=48 * 1024 * 1024),
        cost_estimate=pl.CostEstimate(flops=10 * rows * lb * width * width, bytes_accessed=16 * 2**20, transcendentals=0),
    )(picks.reshape(chunks, CH), archive, first_factor, second_factor, targets)


def plain(archive, picks, first_factor, second_factor, targets, scale):
    rows = picks.shape[0]
    local_blocks = first_factor.shape[0]
    width = first_factor.shape[1]
    x = jnp.take(archive, picks, axis=0).reshape(rows, local_blocks, width)
    y_first = jnp.einsum("sia,iab->ibs", x, first_factor, preferred_element_type=F32).astype(BF16)
    z = lax.all_to_all(y_first, "feat", split_axis=1, concat_axis=0, tiled=True)
    z_float = z.astype(F32)
    hidden = jax.nn.gelu(z_float).astype(BF16)
    pred = jnp.einsum("ijs,jik->sjk", hidden, second_factor, preferred_element_type=F32)
    goal = targets.reshape(rows, local_blocks, width).astype(F32)
    resid = ((pred - goal) * scale).astype(BF16)
    grad_two = jnp.einsum("ijs,sjk->jik", hidden, resid, preferred_element_type=F32)
    d_hidden = jnp.einsum("sjk,jik->ijs", resid, second_factor, preferred_element_type=F32)
    d_z = jax.vjp(jax.nn.gelu, z_float)[1](d_hidden)[0].astype(BF16)
    d_first = lax.all_to_all(d_z, "feat", split_axis=0, concat_axis=1, tiled=True)
    grad_one = jnp.einsum("sia,ibs->iab", x, d_first, preferred_element_type=F32)
    return grad_one, grad_two


def local(archive, picks, first_factor, second_factor, targets):
    rows = picks.shape[0]
    lb, width, _ = first_factor.shape
    n = lax.axis_size("feat")
    dp = lax.axis_size("dp")
    scale = 1.0 / math.sqrt(rows * dp)
    args = (archive, picks, first_factor, second_factor, targets)
    fits = (lb == 8 and n * lb == width and width == 256 and n == 32 and rows % CH == 0
            and archive.shape[0] % CH == 0 and archive.shape[0] <= 1024 and rows <= 512)
    if fits:
        grad_one, grad_two = fused(n, *args, scale)
    else:
        grad_one, grad_two = plain(*args, scale)
    if dp > 1:
        half = width // dp
        offset = lax.axis_index("dp") * half
        one, two = lax.psum((grad_one.astype(BF16), grad_two.astype(BF16)), "dp")
        grad_one = lax.dynamic_slice_in_dim(one.astype(F32), offset, half, 1)
        grad_two = lax.dynamic_slice_in_dim(two.astype(F32), offset, half, 1)
    return grad_one, grad_two


def solution(mesh):
    return jax.shard_map(
        local,
        mesh=mesh,
        in_specs=(
            P("grp", "feat"),
            P(("grp", "dp")),
            P(("grp", "feat"), None, None),
            P(("grp", "feat"), None, None),
            P(("grp", "dp"), "feat"),
        ),
        out_specs=(P(("grp", "feat"), "dp", None), P(("grp", "feat"), "dp", None)),
        check_vma=False,
    )
```

```python
import functools
import math

import jax
import jax.numpy as jnp
from jax import lax
from jax.experimental import pallas as pl
from jax.experimental.pallas import tpu as pltpu
from jax.sharding import PartitionSpec as P

BF16 = jnp.bfloat16
F32 = jnp.float32
CH = 128
FOLDS = (4, 1)
ROOT = math.sqrt(2.0 / math.pi)
CUBE = 0.044715


def dot(a, b, ca, cb):
    return lax.dot_general(a, b, (((ca,), (cb,)), ((), ())), preferred_element_type=F32)


def flip(me, k, n):
    out = 0
    bit = 1
    while bit < n:
        out = out + ((me // bit + k // bit) % 2) * bit
        bit *= 2
    return out


def ranker(picks, place, count):
    chunks = picks.shape[0]
    blocks = place.shape[0]
    lane = lax.broadcasted_iota(jnp.int32, (CH, CH), 1)
    sub = lax.broadcasted_iota(jnp.int32, (CH, CH), 0)
    hits = [jnp.zeros((8, CH), F32) for _ in range(blocks)]
    for c in range(chunks):
        col = jnp.broadcast_to(picks[pl.ds(c, 1), :].astype(F32), (CH, CH)).T.astype(jnp.int32)
        for b in range(blocks):
            hit = (col == lane + b * CH).astype(F32)
            hits[b] = jnp.maximum(hits[b], jnp.max(hit.reshape(CH // 8, 8, CH), axis=0))
    seen = jnp.concatenate([jnp.max(h, axis=0, keepdims=True) for h in hits], axis=0)
    seen_b = seen.astype(BF16)
    before = dot(seen_b, (sub < lane).astype(BF16), 1, 0)
    rows = lax.broadcasted_iota(jnp.int32, (blocks, blocks), 0)
    cols = lax.broadcasted_iota(jnp.int32, (blocks, blocks), 1)
    above = jnp.sum(dot((cols < rows).astype(BF16), seen_b, 1, 0), axis=1, keepdims=True)
    place[...] = jnp.where(seen > 0.5, before + above, -1.0).astype(jnp.int32)
    count[0, 0] = jnp.sum(seen).astype(jnp.int32)


def rank(picks, patterns):
    return pl.pallas_call(
        ranker,
        out_shape=(jax.ShapeDtypeStruct((patterns // CH, CH), jnp.int32), jax.ShapeDtypeStruct((1, 1), jnp.int32)),
        in_specs=[pl.BlockSpec(memory_space=pltpu.VMEM)],
        out_specs=(pl.BlockSpec(memory_space=pltpu.VMEM), pl.BlockSpec(memory_space=pltpu.SMEM)),
    )(picks)


def kernel(n, lb, folds, scale, picks, place, arch_hbm, f1_hbm, f2_hbm, goal_hbm, g1_hbm, g2_hbm,
           arch, f1, f2, goal, f1t, xc, xt, send, recv, bsend, brecv, zbuf, dzbuf, g1, g2, hot, pick_keep,
           in_sem, out_sem, send_sem, recv_sem, bsend_sem, brecv_sem):
    me = lax.axis_index("feat")
    width = n * lb
    rows = goal.shape[0]
    chunks = len(folds)
    patterns = arch.shape[0]
    blocks = patterns // CH
    cell = lb * lb
    per = width // cell
    part = per * lb

    loads = [
        pltpu.make_async_copy(src, dst, in_sem.at[t])
        for t, (src, dst) in enumerate(((f1_hbm, f1), (arch_hbm, arch), (f2_hbm, f2), (goal_hbm, goal)))
    ]
    for load in loads:
        load.start()

    barrier = pltpu.get_barrier_semaphore()

    def greet(k, carry):
        pl.semaphore_signal(barrier, inc=1, device_id={"feat": flip(me, k, n)}, device_id_type=pl.DeviceIdType.MESH)
        return carry

    lax.fori_loop(1, n, greet, 0)

    left = lax.broadcasted_iota(jnp.int32, (width, width), 0)
    right = lax.broadcasted_iota(jnp.int32, (width, width), 1)
    perm = ((right % lb) * part + right // lb == left).astype(BF16)

    def fold_matrix(fold):
        few = lb // fold
        i = right % lb
        return ((i // few) * (n * few) + (right // lb) * few + i % few == left).astype(BF16)

    def chosen(c, q):
        span = CH // folds[c]
        row = lax.broadcasted_iota(jnp.int32, (CH, CH), 0) - q * span
        slot = jnp.where((row >= 0) & (row < span), row + c * CH, -2)
        return jnp.concatenate(
            [(place[pl.ds(b, 1), :] == slot).astype(BF16) for b in range(blocks)], axis=1)

    loads[0].wait()

    def turn(i, carry):
        f1t[i] = f1[i].T
        return carry

    lax.fori_loop(0, lb, turn, 0)
    loads[1].wait()

    def cells(c):
        return pl.ds(0, cell // folds[c])

    def copy_to(sbuf, rbuf, ssem, rsem, c, peer):
        return pltpu.make_async_remote_copy(
            src_ref=sbuf.at[c, peer, cells(c)], dst_ref=rbuf.at[c, me, cells(c)],
            send_sem=ssem.at[c], recv_sem=rsem.at[c],
            device_id={"feat": peer}, device_id_type=pl.DeviceIdType.MESH)

    def send_all(sbuf, rbuf, ssem, rsem, c):
        def one(t, carry):
            copy_to(sbuf, rbuf, ssem, rsem, c, flip(me, n - 1 - t, n)).start()
            return carry

        lax.fori_loop(0, n - 1, one, 0)
        rbuf[c, me, cells(c)] = sbuf[c, me, cells(c)]

    def await_all(buf, sem, c):
        block = buf.at[c, pl.ds(0, n - 1), cells(c)]
        pltpu.make_async_copy(block, block, sem.at[c]).wait()

    for c in range(chunks):
        fold = folds[c]
        few = lb // fold
        for q in range(fold):
            pick_keep[q] = chosen(c, q)

        def forward(p, carry):
            both = []
            for h in range(2):
                y = None
                for q in range(fold):
                    i = q * few + p * 2 + h
                    cols = pl.ds(pl.multiple_of(i * width, width), width)
                    x = dot(pick_keep[q], arch[:, cols], 1, 0).astype(BF16)
                    xc[i] = x
                    term = dot(f1t[i], x, 1, 1)
                    y = term if y is None else y + term
                both.append(y.reshape(n, lb, CH))
            at = pl.ds(pl.multiple_of(p * 2 * lb, 2 * lb), 2 * lb)
            send[c, :, at, :] = jnp.concatenate(both, axis=1).astype(BF16)
            return carry

        lax.fori_loop(0, few // 2, forward, 0)
        if c == 0:
            pl.semaphore_wait(barrier, n - 1)
        send_all(send, recv, send_sem, recv_sem, c)

        def turn_x(i, carry):
            xt[c, i] = xc[i].T
            return carry

        lax.fori_loop(0, lb, turn_x, 0)

    for c in range(rows // CH):
        col = jnp.broadcast_to(picks[pl.ds(c, 1), :].astype(F32), (CH, CH)).T.astype(jnp.int32)
        lane = lax.broadcasted_iota(jnp.int32, (CH, CH), 1)
        for b in range(blocks):
            hot[c * CH:(c + 1) * CH, b * CH:(b + 1) * CH] = (col == lane + b * CH).astype(BF16)

    loads[2].wait()
    loads[3].wait()

    for c in range(chunks):
        fold = folds[c]
        span = CH // fold
        tall = width // fold
        member = dot(chosen(c, 0), hot[...], 1, 1)
        times = jnp.sum(member, axis=1, keepdims=True)
        member = member.astype(BF16)
        many = per * fold
        await_all(recv, recv_sem, c)

        def permute(g, carry):
            got = recv[c, pl.ds(g * many, many), cells(c)].reshape(width, CH)
            z = dot(perm, got, 1, 0).reshape(lb, part, CH)
            zbuf[:, pl.ds(pl.multiple_of(g * part, part), part), :] = z
            return carry

        lax.fori_loop(0, n // many, permute, 0)

        def middle(j, carry):
            if fold == 1:
                z = zbuf[j]
            else:
                flat = zbuf[j, pl.ds(0, tall), :]
                pieces = [flat if q == 0 else pltpu.roll(flat, CH - q * span, 1) for q in range(fold)]
                z = dot(fold_matrix(fold), jnp.concatenate(pieces, axis=0).astype(BF16), 0, 0)
            sq = z * z
            t = jnp.tanh(ROOT * z * (1.0 + CUBE * sq))
            half = 0.5 * (1.0 + t)
            hidden = (z * half).astype(BF16)
            slope = half + 0.5 * z * (1.0 - t * t) * (ROOT * (1.0 + 3.0 * CUBE * sq))
            pred = dot(hidden, f2[j], 0, 0)
            cols = pl.ds(pl.multiple_of(j * width, width), width)
            want = dot(member, goal[:, cols], 1, 0)
            resid = ((times * pred - want) * scale).astype(BF16)
            grad = dot(hidden, resid, 1, 0)
            if c == 0:
                g2[j] = grad
            else:
                g2[j] += grad
            dh = dot(f2[j], resid, 1, 1)
            dz = (dh * slope).astype(BF16)
            if fold == 1:
                dzbuf[j] = dz
            else:
                flat = dot(fold_matrix(fold), dz, 1, 0)
                total = flat[:tall]
                for q in range(1, fold):
                    total = total + pltpu.roll(flat[q * tall:(q + 1) * tall], q * span, 1)
                dzbuf[j, pl.ds(0, tall), :] = total.astype(BF16)
            return carry

        lax.fori_loop(0, lb, middle, 0)

        def back(g, carry):
            rows_in = dzbuf[:, pl.ds(pl.multiple_of(g * part, part), part), :].reshape(width, CH)
            out = dot(perm, rows_in, 0, 0).astype(BF16)
            bsend[c, pl.ds(g * many, many), cells(c)] = out.reshape(many, cell // fold, CH)
            return carry

        lax.fori_loop(0, n // many, back, 0)
        send_all(bsend, brecv, bsend_sem, brecv_sem, c)

    out2 = pltpu.make_async_copy(g2, g2_hbm, out_sem.at[0])
    out2.start()

    for c in range(chunks):
        fold = folds[c]
        few = lb // fold
        await_all(brecv, brecv_sem, c)

        def last(p, carry):
            at = pl.ds(pl.multiple_of(p * 2 * lb, 2 * lb), 2 * lb)
            both = brecv[c, :, at, :].astype(F32)
            for h in range(2):
                d = both[:, h * lb:(h + 1) * lb, :].reshape(width, CH).astype(BF16)
                for q in range(fold):
                    i = q * few + p * 2 + h
                    grad = dot(xt[c, i], d, 1, 1)
                    if c == 0:
                        g1[i] = grad
                    else:
                        g1[i] += grad
            return carry

        lax.fori_loop(0, few // 2, last, 0)

    out1 = pltpu.make_async_copy(g1, g1_hbm, out_sem.at[1])
    out1.start()
    for c in range(chunks):
        await_all(send, send_sem, c)
        await_all(bsend, bsend_sem, c)
    out2.wait()
    out1.wait()


def fused(n, scale, which, folds, picks, place, archive, first_factor, second_factor, targets):
    rows = targets.shape[0]
    lb, width, _ = first_factor.shape
    chunks = len(folds)
    any_ = pl.BlockSpec(memory_space=pl.ANY)
    grads = jax.ShapeDtypeStruct((lb, width, width), F32)
    block = pltpu.VMEM((chunks, n, lb * lb, CH), BF16)
    dma = pltpu.SemaphoreType.DMA
    return pl.pallas_call(
        functools.partial(kernel, n, lb, folds, scale),
        out_shape=(grads, grads),
        in_specs=[pl.BlockSpec(memory_space=pltpu.VMEM)] * 2 + [any_] * 4,
        out_specs=(any_, any_),
        scratch_shapes=[
            pltpu.VMEM(archive.shape, BF16),
            pltpu.VMEM(first_factor.shape, BF16),
            pltpu.VMEM(second_factor.shape, BF16),
            pltpu.VMEM(targets.shape, BF16),
            pltpu.VMEM(first_factor.shape, BF16),
            pltpu.VMEM((lb, CH, width), BF16),
            pltpu.VMEM((chunks, lb, width, CH), BF16),
            block, block, block, block,
            pltpu.VMEM((lb, width, CH), F32),
            pltpu.VMEM((lb, width, CH), BF16),
            pltpu.VMEM((lb, width, width), F32),
            pltpu.VMEM((lb, width, width), F32),
            pltpu.VMEM((rows, archive.shape[0]), BF16),
            pltpu.VMEM((max(folds), CH, archive.shape[0]), BF16),
            dma((4,)), dma((2,)),
            dma((chunks,)), dma((chunks,)), dma((chunks,)), dma((chunks,)),
        ],
        compiler_params=pltpu.CompilerParams(
            collective_id=which, has_side_effects=True, vmem_limit_bytes=60 * 1024 * 1024),
        cost_estimate=pl.CostEstimate(flops=10 * rows * lb * width * width, bytes_accessed=16 * 2**20, transcendentals=0),
    )(picks, place, archive, first_factor, second_factor, targets)


def distinct(n, scale, archive, picks, first_factor, second_factor, targets):
    chunks = picks.shape[0] // CH
    picks = picks.reshape(chunks, CH)
    place, count = rank(picks, archive.shape[0])
    count = count[0, 0]
    if lax.axis_size("grp") * lax.axis_size("dp") > 1:
        count = lax.pmax(count, ("grp", "dp"))
    plans = [(1,) * (chunks - 1) + (fold,) for fold in FOLDS]
    index = 0
    for folds in plans[:-1]:
        index = index + (count > sum(CH // fold for fold in folds)).astype(jnp.int32)
    calls = [functools.partial(fused, n, scale, which, folds) for which, folds in enumerate(plans)]
    return lax.switch(index, calls, picks, place, archive, first_factor, second_factor, targets)


def plain(archive, picks, first_factor, second_factor, targets, scale):
    rows = picks.shape[0]
    local_blocks = first_factor.shape[0]
    width = first_factor.shape[1]
    x = jnp.take(archive, picks, axis=0).reshape(rows, local_blocks, width)
    y_first = jnp.einsum("sia,iab->ibs", x, first_factor, preferred_element_type=F32).astype(BF16)
    z = lax.all_to_all(y_first, "feat", split_axis=1, concat_axis=0, tiled=True)
    z_float = z.astype(F32)
    hidden = jax.nn.gelu(z_float).astype(BF16)
    pred = jnp.einsum("ijs,jik->sjk", hidden, second_factor, preferred_element_type=F32)
    goal = targets.reshape(rows, local_blocks, width).astype(F32)
    resid = ((pred - goal) * scale).astype(BF16)
    grad_two = jnp.einsum("ijs,sjk->jik", hidden, resid, preferred_element_type=F32)
    d_hidden = jnp.einsum("sjk,jik->ijs", resid, second_factor, preferred_element_type=F32)
    d_z = jax.vjp(jax.nn.gelu, z_float)[1](d_hidden)[0].astype(BF16)
    d_first = lax.all_to_all(d_z, "feat", split_axis=0, concat_axis=1, tiled=True)
    grad_one = jnp.einsum("sia,ibs->iab", x, d_first, preferred_element_type=F32)
    return grad_one, grad_two


def local(archive, picks, first_factor, second_factor, targets):
    rows = picks.shape[0]
    lb, width, _ = first_factor.shape
    n = lax.axis_size("feat")
    dp = lax.axis_size("dp")
    scale = 1.0 / math.sqrt(rows * dp)
    args = (archive, picks, first_factor, second_factor, targets)
    fits = (lb == 8 and n * lb == width and width == 256 and n == 32 and rows % CH == 0
            and archive.shape[0] % CH == 0 and archive.shape[0] <= 1024 and rows <= 512)
    if fits:
        grad_one, grad_two = distinct(n, scale, *args)
    else:
        grad_one, grad_two = plain(*args, scale)
    if dp > 1:
        half = width // dp
        offset = lax.axis_index("dp") * half
        one, two = lax.psum((grad_one.astype(BF16), grad_two.astype(BF16)), "dp")
        grad_one = lax.dynamic_slice_in_dim(one.astype(F32), offset, half, 1)
        grad_two = lax.dynamic_slice_in_dim(two.astype(F32), offset, half, 1)
    return grad_one, grad_two


def solution(mesh):
    return jax.shard_map(
        local,
        mesh=mesh,
        in_specs=(
            P("grp", "feat"),
            P(("grp", "dp")),
            P(("grp", "feat"), None, None),
            P(("grp", "feat"), None, None),
            P(("grp", "dp"), "feat"),
        ),
        out_specs=(P(("grp", "feat"), "dp", None), P(("grp", "feat"), "dp", None)),
        check_vma=False,
    )
```

```python
import functools
import math

import jax
import jax.numpy as jnp
from jax import lax
from jax.experimental import pallas as pl
from jax.experimental.pallas import tpu as pltpu
from jax.sharding import PartitionSpec as P

BF16 = jnp.bfloat16
F32 = jnp.float32
CH = 128
FOLDS = (4, 1)
ROOT = math.sqrt(2.0 / math.pi)
CUBE = 0.044715


def dot(a, b, ca, cb):
    return lax.dot_general(a, b, (((ca,), (cb,)), ((), ())), preferred_element_type=F32)


def flip(me, k, n):
    out = 0
    bit = 1
    while bit < n:
        out = out + ((me // bit + k // bit) % 2) * bit
        bit *= 2
    return out


def ranker(picks, place, count):
    chunks = picks.shape[0]
    blocks = place.shape[0]
    lane = lax.broadcasted_iota(jnp.int32, (CH, CH), 1)
    sub = lax.broadcasted_iota(jnp.int32, (CH, CH), 0)
    hits = [jnp.zeros((8, CH), F32) for _ in range(blocks)]
    for c in range(chunks):
        col = jnp.broadcast_to(picks[pl.ds(c, 1), :].astype(F32), (CH, CH)).T.astype(jnp.int32)
        for b in range(blocks):
            hit = (col == lane + b * CH).astype(F32)
            hits[b] = jnp.maximum(hits[b], jnp.max(hit.reshape(CH // 8, 8, CH), axis=0))
    seen = jnp.concatenate([jnp.max(h, axis=0, keepdims=True) for h in hits], axis=0)
    seen_b = seen.astype(BF16)
    before = dot(seen_b, (sub < lane).astype(BF16), 1, 0)
    rows = lax.broadcasted_iota(jnp.int32, (blocks, blocks), 0)
    cols = lax.broadcasted_iota(jnp.int32, (blocks, blocks), 1)
    above = jnp.sum(dot((cols < rows).astype(BF16), seen_b, 1, 0), axis=1, keepdims=True)
    place[...] = jnp.where(seen > 0.5, before + above, -1.0).astype(jnp.int32)
    count[0, 0] = jnp.sum(seen).astype(jnp.int32)


def rank(picks, patterns):
    return pl.pallas_call(
        ranker,
        out_shape=(jax.ShapeDtypeStruct((patterns // CH, CH), jnp.int32), jax.ShapeDtypeStruct((1, 1), jnp.int32)),
        in_specs=[pl.BlockSpec(memory_space=pltpu.VMEM)],
        out_specs=(pl.BlockSpec(memory_space=pltpu.VMEM), pl.BlockSpec(memory_space=pltpu.SMEM)),
    )(picks)


def kernel(n, lb, folds, scale, picks, place, arch_hbm, f1_hbm, f2_hbm, goal_hbm, g1_hbm, g2_hbm,
           arch, f1, f2, goal, f1t, xc, xt, send, recv, bsend, brecv, zbuf, dzbuf, g1, g2, g1b, g2b, hot, pick_keep,
           in_sem, f1_sem, arch_sem, out_sem, send_sem, recv_sem, bsend_sem, brecv_sem):
    me = lax.axis_index("feat")
    width = n * lb
    rows = goal.shape[0]
    chunks = len(folds)
    patterns = arch.shape[0]
    blocks = patterns // CH
    cell = lb * lb
    per = width // cell
    part = per * lb

    def load_pair(p):
        some = pl.ds(p * 2, 2)
        cols = pl.ds(pl.multiple_of(p * 2 * width, 2 * width), 2 * width)
        return (pltpu.make_async_copy(f1_hbm.at[some], f1.at[some], f1_sem.at[p]),
                pltpu.make_async_copy(arch_hbm.at[:, cols], arch.at[:, cols], arch_sem.at[p]))

    loads = [
        pltpu.make_async_copy(src, dst, in_sem.at[t])
        for t, (src, dst) in enumerate(((f2_hbm, f2), (goal_hbm, goal)))
    ]
    for p in range(lb // 2):
        for load in load_pair(p):
            load.start()
    for load in loads:
        load.start()

    barrier = pltpu.get_barrier_semaphore()

    def greet(k, carry):
        pl.semaphore_signal(barrier, inc=1, device_id={"feat": flip(me, k, n)}, device_id_type=pl.DeviceIdType.MESH)
        return carry

    lax.fori_loop(1, n, greet, 0)

    left = lax.broadcasted_iota(jnp.int32, (width, width), 0)
    right = lax.broadcasted_iota(jnp.int32, (width, width), 1)
    perm = ((right % lb) * part + right // lb == left).astype(BF16)

    def fold_matrix(fold):
        few = lb // fold
        i = right % lb
        return ((i // few) * (n * few) + (right // lb) * few + i % few == left).astype(BF16)

    def chosen(c, q):
        span = CH // folds[c]
        row = lax.broadcasted_iota(jnp.int32, (CH, CH), 0) - q * span
        slot = jnp.where((row >= 0) & (row < span), row + c * CH, -2)
        return jnp.concatenate(
            [(place[pl.ds(b, 1), :] == slot).astype(BF16) for b in range(blocks)], axis=1)

    def cells(c):
        return pl.ds(0, cell // folds[c])

    def copy_to(sbuf, rbuf, ssem, rsem, c, peer, at):
        return pltpu.make_async_remote_copy(
            src_ref=sbuf.at[c, peer, at], dst_ref=rbuf.at[c, me, at],
            send_sem=ssem.at[c], recv_sem=rsem.at[c],
            device_id={"feat": peer}, device_id_type=pl.DeviceIdType.MESH)

    def send_all(sbuf, rbuf, ssem, rsem, c, at):
        def one(t, carry):
            peer = flip(me, n - 1 - t // 2 - (t % 2) * (n // 2), n)
            copy_to(sbuf, rbuf, ssem, rsem, c, peer, at).start()
            return carry

        lax.fori_loop(0, n - 1, one, 0)
        rbuf[c, me, at] = sbuf[c, me, at]

    def await_all(buf, sem, c):
        block = buf.at[c, pl.ds(0, n - 1), cells(c)]
        pltpu.make_async_copy(block, block, sem.at[c]).wait()

    for c in range(chunks):
        fold = folds[c]
        few = lb // fold
        for q in range(fold):
            pick_keep[q] = chosen(c, q)

        def forward(p, carry):
            both = []
            if c == 0:
                for load in load_pair(p):
                    load.wait()
                for h in range(2):
                    f1t[p * 2 + h] = f1[p * 2 + h].T
            for h in range(2):
                y = None
                for q in range(fold):
                    i = q * few + p * 2 + h
                    cols = pl.ds(pl.multiple_of(i * width, width), width)
                    x = dot(pick_keep[q], arch[:, cols], 1, 0).astype(BF16)
                    xc[i] = x
                    term = dot(f1t[i], x, 1, 1)
                    y = term if y is None else y + term
                both.append(y.reshape(n, lb, CH))
            at = pl.ds(pl.multiple_of(p * 2 * lb, 2 * lb), 2 * lb)
            send[c, :, at, :] = jnp.concatenate(both, axis=1).astype(BF16)
            if c == 0:
                send_all(send, recv, send_sem, recv_sem, c, at)
            return carry

        if c == 0:
            pl.semaphore_wait(barrier, n - 1)
        lax.fori_loop(0, few // 2, forward, 0)
        if c > 0:
            send_all(send, recv, send_sem, recv_sem, c, cells(c))

        def turn_x(i, carry):
            xt[c, i] = xc[i].T
            return carry

        lax.fori_loop(0, lb, turn_x, 0)

    for c in range(rows // CH):
        col = jnp.broadcast_to(picks[pl.ds(c, 1), :].astype(F32), (CH, CH)).T.astype(jnp.int32)
        lane = lax.broadcasted_iota(jnp.int32, (CH, CH), 1)
        for b in range(blocks):
            hot[c * CH:(c + 1) * CH, b * CH:(b + 1) * CH] = (col == lane + b * CH).astype(BF16)

    loads[0].wait()
    loads[1].wait()

    for c in range(chunks):
        fold = folds[c]
        span = CH // fold
        tall = width // fold
        member = dot(chosen(c, 0), hot[...], 1, 1)
        times = jnp.sum(member, axis=1, keepdims=True)
        member = member.astype(BF16)
        many = per * fold
        await_all(recv, recv_sem, c)

        def permute(g, carry):
            got = recv[c, pl.ds(g * many, many), cells(c)].reshape(width, CH)
            z = dot(perm, got, 1, 0).reshape(lb, part, CH)
            zbuf[:, pl.ds(pl.multiple_of(g * part, part), part), :] = z
            return carry

        lax.fori_loop(0, n // many, permute, 0)

        def middle(j, carry):
            if fold == 1:
                z = zbuf[j]
            else:
                flat = zbuf[j, pl.ds(0, tall), :]
                pieces = [flat if q == 0 else pltpu.roll(flat, CH - q * span, 1) for q in range(fold)]
                z = dot(fold_matrix(fold), jnp.concatenate(pieces, axis=0).astype(BF16), 0, 0)
            sq = z * z
            t = jnp.tanh(ROOT * z * (1.0 + CUBE * sq))
            half = 0.5 * (1.0 + t)
            hidden = (z * half).astype(BF16)
            slope = half + 0.5 * z * (1.0 - t * t) * (ROOT * (1.0 + 3.0 * CUBE * sq))
            pred = dot(hidden, f2[j], 0, 0)
            cols = pl.ds(pl.multiple_of(j * width, width), width)
            want = dot(member, goal[:, cols], 1, 0)
            resid = ((times * pred - want) * scale).astype(BF16)
            grad = dot(hidden, resid, 1, 0)
            total = grad if c == 0 else g2[j] + grad
            if c < chunks - 1:
                g2[j] = total
            else:
                g2b[j] = total.astype(BF16)
            dh = dot(f2[j], resid, 1, 1)
            dz = (dh * slope).astype(BF16)
            if fold == 1:
                dzbuf[j] = dz
            else:
                flat = dot(fold_matrix(fold), dz, 1, 0)
                folded = flat[:tall]
                for q in range(1, fold):
                    folded = folded + pltpu.roll(flat[q * tall:(q + 1) * tall], q * span, 1)
                dzbuf[j, pl.ds(0, tall), :] = folded.astype(BF16)
            return carry

        lax.fori_loop(0, lb, middle, 0)

        def back(g, carry):
            rows_in = dzbuf[:, pl.ds(pl.multiple_of(g * part, part), part), :].reshape(width, CH)
            out = dot(perm, rows_in, 0, 0).astype(BF16)
            bsend[c, pl.ds(g * many, many), cells(c)] = out.reshape(many, cell // fold, CH)
            return carry

        lax.fori_loop(0, n // many, back, 0)
        send_all(bsend, brecv, bsend_sem, brecv_sem, c, cells(c))

    out2 = pltpu.make_async_copy(g2b, g2_hbm, out_sem.at[0])
    out2.start()

    for c in range(chunks):
        fold = folds[c]
        few = lb // fold
        await_all(brecv, brecv_sem, c)

        def last(p, carry):
            at = pl.ds(pl.multiple_of(p * 2 * lb, 2 * lb), 2 * lb)
            both = brecv[c, :, at, :].astype(F32)
            for h in range(2):
                d = both[:, h * lb:(h + 1) * lb, :].reshape(width, CH).astype(BF16)
                for q in range(fold):
                    i = q * few + p * 2 + h
                    grad = dot(xt[c, i], d, 1, 1)
                    total = grad if c == 0 else g1[i] + grad
                    if c < chunks - 1:
                        g1[i] = total
                    else:
                        g1b[i] = total.astype(BF16)
            return carry

        lax.fori_loop(0, few // 2, last, 0)

    out1 = pltpu.make_async_copy(g1b, g1_hbm, out_sem.at[1])
    out1.start()
    for c in range(chunks):
        await_all(send, send_sem, c)
        await_all(bsend, bsend_sem, c)
    out2.wait()
    out1.wait()


def fused(n, scale, which, folds, picks, place, archive, first_factor, second_factor, targets):
    rows = targets.shape[0]
    lb, width, _ = first_factor.shape
    chunks = len(folds)
    any_ = pl.BlockSpec(memory_space=pl.ANY)
    grads = jax.ShapeDtypeStruct((lb, width, width), BF16)
    block = pltpu.VMEM((chunks, n, lb * lb, CH), BF16)
    dma = pltpu.SemaphoreType.DMA
    return pl.pallas_call(
        functools.partial(kernel, n, lb, folds, scale),
        out_shape=(grads, grads),
        in_specs=[pl.BlockSpec(memory_space=pltpu.VMEM)] * 2 + [any_] * 4,
        out_specs=(any_, any_),
        scratch_shapes=[
            pltpu.VMEM(archive.shape, BF16),
            pltpu.VMEM(first_factor.shape, BF16),
            pltpu.VMEM(second_factor.shape, BF16),
            pltpu.VMEM(targets.shape, BF16),
            pltpu.VMEM(first_factor.shape, BF16),
            pltpu.VMEM((lb, CH, width), BF16),
            pltpu.VMEM((chunks, lb, width, CH), BF16),
            block, block, block, block,
            pltpu.VMEM((lb, width, CH), F32),
            pltpu.VMEM((lb, width, CH), BF16),
            pltpu.VMEM((lb, width, width), F32),
            pltpu.VMEM((lb, width, width), F32),
            pltpu.VMEM(first_factor.shape, BF16),
            pltpu.VMEM(first_factor.shape, BF16),
            pltpu.VMEM((rows, archive.shape[0]), BF16),
            pltpu.VMEM((max(folds), CH, archive.shape[0]), BF16),
            dma((2,)), dma((lb // 2,)), dma((lb // 2,)), dma((2,)),
            dma((chunks,)), dma((chunks,)), dma((chunks,)), dma((chunks,)),
        ],
        compiler_params=pltpu.CompilerParams(
            collective_id=which, has_side_effects=True, vmem_limit_bytes=60 * 1024 * 1024),
        cost_estimate=pl.CostEstimate(flops=10 * rows * lb * width * width, bytes_accessed=16 * 2**20, transcendentals=0),
    )(picks, place, archive, first_factor, second_factor, targets)


def distinct(n, scale, archive, picks, first_factor, second_factor, targets):
    chunks = picks.shape[0] // CH
    picks = picks.reshape(chunks, CH)
    place, count = rank(picks, archive.shape[0])
    count = count[0, 0]
    if lax.axis_size("grp") * lax.axis_size("dp") > 1:
        count = lax.pmax(count, ("grp", "dp"))
    plans = [(1,) * (chunks - 1) + (fold,) for fold in FOLDS]
    index = 0
    for folds in plans[:-1]:
        index = index + (count > sum(CH // fold for fold in folds)).astype(jnp.int32)
    calls = [functools.partial(fused, n, scale, which, folds) for which, folds in enumerate(plans)]
    one, two = lax.switch(index, calls, picks, place, archive, first_factor, second_factor, targets)
    return one.astype(F32), two.astype(F32)


def plain(archive, picks, first_factor, second_factor, targets, scale):
    rows = picks.shape[0]
    local_blocks = first_factor.shape[0]
    width = first_factor.shape[1]
    x = jnp.take(archive, picks, axis=0).reshape(rows, local_blocks, width)
    y_first = jnp.einsum("sia,iab->ibs", x, first_factor, preferred_element_type=F32).astype(BF16)
    z = lax.all_to_all(y_first, "feat", split_axis=1, concat_axis=0, tiled=True)
    z_float = z.astype(F32)
    hidden = jax.nn.gelu(z_float).astype(BF16)
    pred = jnp.einsum("ijs,jik->sjk", hidden, second_factor, preferred_element_type=F32)
    goal = targets.reshape(rows, local_blocks, width).astype(F32)
    resid = ((pred - goal) * scale).astype(BF16)
    grad_two = jnp.einsum("ijs,sjk->jik", hidden, resid, preferred_element_type=F32)
    d_hidden = jnp.einsum("sjk,jik->ijs", resid, second_factor, preferred_element_type=F32)
    d_z = jax.vjp(jax.nn.gelu, z_float)[1](d_hidden)[0].astype(BF16)
    d_first = lax.all_to_all(d_z, "feat", split_axis=0, concat_axis=1, tiled=True)
    grad_one = jnp.einsum("sia,ibs->iab", x, d_first, preferred_element_type=F32)
    return grad_one, grad_two


def local(archive, picks, first_factor, second_factor, targets):
    rows = picks.shape[0]
    lb, width, _ = first_factor.shape
    n = lax.axis_size("feat")
    dp = lax.axis_size("dp")
    scale = 1.0 / math.sqrt(rows * dp)
    args = (archive, picks, first_factor, second_factor, targets)
    fits = (lb == 8 and n * lb == width and width == 256 and n == 32 and rows % CH == 0
            and archive.shape[0] % CH == 0 and archive.shape[0] <= 1024 and rows <= 512)
    if fits:
        grad_one, grad_two = distinct(n, scale, *args)
    else:
        grad_one, grad_two = plain(*args, scale)
    if dp > 1:
        half = width // dp
        offset = lax.axis_index("dp") * half
        one, two = lax.psum((grad_one.astype(BF16), grad_two.astype(BF16)), "dp")
        grad_one = lax.dynamic_slice_in_dim(one.astype(F32), offset, half, 1)
        grad_two = lax.dynamic_slice_in_dim(two.astype(F32), offset, half, 1)
    return grad_one, grad_two


def solution(mesh):
    return jax.shard_map(
        local,
        mesh=mesh,
        in_specs=(
            P("grp", "feat"),
            P(("grp", "dp")),
            P(("grp", "feat"), None, None),
            P(("grp", "feat"), None, None),
            P(("grp", "dp"), "feat"),
        ),
        out_specs=(P(("grp", "feat"), "dp", None), P(("grp", "feat"), "dp", None)),
        check_vma=False,
    )
```

```python
import functools
import math

import jax
import jax.numpy as jnp
from jax import lax
from jax.experimental import pallas as pl
from jax.experimental.pallas import tpu as pltpu
from jax.sharding import PartitionSpec as P

BF16 = jnp.bfloat16
F32 = jnp.float32
CH = 128
FOLDS = (4, 1)
ROOT = math.sqrt(2.0 / math.pi)
CUBE = 0.044715


def dot(a, b, ca, cb):
    return lax.dot_general(a, b, (((ca,), (cb,)), ((), ())), preferred_element_type=F32)


def flip(me, k, n):
    out = 0
    bit = 1
    while bit < n:
        out = out + ((me // bit + k // bit) % 2) * bit
        bit *= 2
    return out


def ranker(picks, place, count):
    chunks = picks.shape[0]
    blocks = place.shape[0]
    lane = lax.broadcasted_iota(jnp.int32, (CH, CH), 1)
    sub = lax.broadcasted_iota(jnp.int32, (CH, CH), 0)
    hits = [jnp.zeros((8, CH), F32) for _ in range(blocks)]
    for c in range(chunks):
        col = jnp.broadcast_to(picks[pl.ds(c, 1), :].astype(F32), (CH, CH)).T.astype(jnp.int32)
        for b in range(blocks):
            hit = (col == lane + b * CH).astype(F32)
            hits[b] = jnp.maximum(hits[b], jnp.max(hit.reshape(CH // 8, 8, CH), axis=0))
    seen = jnp.concatenate([jnp.max(h, axis=0, keepdims=True) for h in hits], axis=0)
    seen_b = seen.astype(BF16)
    before = dot(seen_b, (sub < lane).astype(BF16), 1, 0)
    rows = lax.broadcasted_iota(jnp.int32, (blocks, blocks), 0)
    cols = lax.broadcasted_iota(jnp.int32, (blocks, blocks), 1)
    above = jnp.sum(dot((cols < rows).astype(BF16), seen_b, 1, 0), axis=1, keepdims=True)
    place[...] = jnp.where(seen > 0.5, before + above, -1.0).astype(jnp.int32)
    count[0, 0] = jnp.sum(seen).astype(jnp.int32)


def rank(picks, patterns):
    return pl.pallas_call(
        ranker,
        out_shape=(jax.ShapeDtypeStruct((patterns // CH, CH), jnp.int32), jax.ShapeDtypeStruct((1, 1), jnp.int32)),
        in_specs=[pl.BlockSpec(memory_space=pltpu.VMEM)],
        out_specs=(pl.BlockSpec(memory_space=pltpu.VMEM), pl.BlockSpec(memory_space=pltpu.SMEM)),
    )(picks)


def kernel(n, lb, folds, scale, picks, place, arch_hbm, f1_hbm, f2_hbm, goal_hbm, g1_hbm, g2_hbm,
           arch, f1, f2, goal, f1t, xc, xt, send, recv, bsend, brecv, zbuf, dzbuf, g1, g2, g1b, g2b, hot, pick_keep,
           in_sem, f1_sem, arch_sem, out_sem, send_sem, recv_sem, bsend_sem, brecv_sem):
    me = lax.axis_index("feat")
    width = n * lb
    rows = goal.shape[0]
    chunks = len(folds)
    patterns = arch.shape[0]
    blocks = patterns // CH
    cell = lb * lb
    per = width // cell
    part = per * lb

    def load_pair(p):
        some = pl.ds(p * 2, 2)
        cols = pl.ds(pl.multiple_of(p * 2 * width, 2 * width), 2 * width)
        return (pltpu.make_async_copy(f1_hbm.at[some], f1.at[some], f1_sem.at[p]),
                pltpu.make_async_copy(arch_hbm.at[:, cols], arch.at[:, cols], arch_sem.at[p]))

    loads = [
        pltpu.make_async_copy(src, dst, in_sem.at[t])
        for t, (src, dst) in enumerate(((f2_hbm, f2), (goal_hbm, goal)))
    ]
    for p in range(lb // 2):
        for load in load_pair(p):
            load.start()
    for load in loads:
        load.start()

    barrier = pltpu.get_barrier_semaphore()

    def greet(k, carry):
        pl.semaphore_signal(barrier, inc=1, device_id={"feat": flip(me, k, n)}, device_id_type=pl.DeviceIdType.MESH)
        return carry

    lax.fori_loop(1, n, greet, 0)

    left = lax.broadcasted_iota(jnp.int32, (width, width), 0)
    right = lax.broadcasted_iota(jnp.int32, (width, width), 1)
    perm = ((right % lb) * part + right // lb == left).astype(BF16)

    def fold_matrix(fold):
        few = lb // fold
        i = right % lb
        return ((i // few) * (n * few) + (right // lb) * few + i % few == left).astype(BF16)

    def chosen(c, q):
        span = CH // folds[c]
        row = lax.broadcasted_iota(jnp.int32, (CH, CH), 0) - q * span
        slot = jnp.where((row >= 0) & (row < span), row + c * CH, -2)
        return jnp.concatenate(
            [(place[pl.ds(b, 1), :] == slot).astype(BF16) for b in range(blocks)], axis=1)

    def cells(c):
        return pl.ds(0, cell // folds[c])

    def copy_to(sbuf, rbuf, ssem, rsem, c, peer, at):
        return pltpu.make_async_remote_copy(
            src_ref=sbuf.at[c, peer, at], dst_ref=rbuf.at[c, me, at],
            send_sem=ssem.at[c], recv_sem=rsem.at[c],
            device_id={"feat": peer}, device_id_type=pl.DeviceIdType.MESH)

    def send_some(sbuf, rbuf, ssem, rsem, c, at, low, high):
        def one(t, carry):
            peer = flip(me, n - 1 - t // 2 - (t % 2) * (n // 2), n)
            copy_to(sbuf, rbuf, ssem, rsem, c, peer, at).start()
            return carry

        lax.fori_loop(low, high, one, 0)

    first = (send, recv, send_sem, recv_sem)
    second = (bsend, brecv, bsend_sem, brecv_sem)

    def keep_own(ways, c, at):
        ways[1][c, me, at] = ways[0][c, me, at]

    def feed(waiting, step, steps):
        if waiting is None:
            return
        ways, c = waiting
        each = -(-(n - 1) // steps)
        low = jnp.minimum(step * each, n - 1)
        send_some(*ways, c, cells(c), low, jnp.minimum(low + each, n - 1))

    def await_all(buf, sem, c):
        block = buf.at[c, pl.ds(0, n - 1), cells(c)]
        pltpu.make_async_copy(block, block, sem.at[c]).wait()

    waiting = None
    for c in range(chunks):
        fold = folds[c]
        few = lb // fold
        for q in range(fold):
            pick_keep[q] = chosen(c, q)

        def forward(p, carry):
            both = []
            if c == 0:
                for load in load_pair(p):
                    load.wait()
                for h in range(2):
                    f1t[p * 2 + h] = f1[p * 2 + h].T
            for h in range(2):
                y = None
                for q in range(fold):
                    i = q * few + p * 2 + h
                    cols = pl.ds(pl.multiple_of(i * width, width), width)
                    x = dot(pick_keep[q], arch[:, cols], 1, 0).astype(BF16)
                    xc[i] = x
                    term = dot(f1t[i], x, 1, 1)
                    y = term if y is None else y + term
                both.append(y.reshape(n, lb, CH))
            at = pl.ds(pl.multiple_of(p * 2 * lb, 2 * lb), 2 * lb)
            send[c, :, at, :] = jnp.concatenate(both, axis=1).astype(BF16)
            if c == 0:
                send_some(*first, c, at, 0, n - 1)
            else:
                feed(waiting, p, few // 2)
            return carry

        if c == 0:
            pl.semaphore_wait(barrier, n - 1)
        lax.fori_loop(0, few // 2, forward, 0)
        keep_own(first, c, cells(c))
        waiting = (first, c) if c > 0 else None

        def turn_x(i, carry):
            xt[c, i] = xc[i].T
            return carry

        lax.fori_loop(0, lb, turn_x, 0)

    for c in range(rows // CH):
        col = jnp.broadcast_to(picks[pl.ds(c, 1), :].astype(F32), (CH, CH)).T.astype(jnp.int32)
        lane = lax.broadcasted_iota(jnp.int32, (CH, CH), 1)
        for b in range(blocks):
            hot[c * CH:(c + 1) * CH, b * CH:(b + 1) * CH] = (col == lane + b * CH).astype(BF16)

    loads[0].wait()
    loads[1].wait()

    for c in range(chunks):
        fold = folds[c]
        span = CH // fold
        tall = width // fold
        member = dot(chosen(c, 0), hot[...], 1, 1)
        times = jnp.sum(member, axis=1, keepdims=True)
        member = member.astype(BF16)
        many = per * fold
        await_all(recv, recv_sem, c)

        def permute(g, carry):
            got = recv[c, pl.ds(g * many, many), cells(c)].reshape(width, CH)
            z = dot(perm, got, 1, 0).reshape(lb, part, CH)
            zbuf[:, pl.ds(pl.multiple_of(g * part, part), part), :] = z
            return carry

        lax.fori_loop(0, n // many, permute, 0)

        def middle(j, carry):
            feed(waiting, j, lb)
            if fold == 1:
                z = zbuf[j]
            else:
                flat = zbuf[j, pl.ds(0, tall), :]
                pieces = [flat if q == 0 else pltpu.roll(flat, CH - q * span, 1) for q in range(fold)]
                z = dot(fold_matrix(fold), jnp.concatenate(pieces, axis=0).astype(BF16), 0, 0)
            sq = z * z
            t = jnp.tanh(ROOT * z * (1.0 + CUBE * sq))
            half = 0.5 * (1.0 + t)
            hidden = (z * half).astype(BF16)
            slope = half + 0.5 * z * (1.0 - t * t) * (ROOT * (1.0 + 3.0 * CUBE * sq))
            pred = dot(hidden, f2[j], 0, 0)
            cols = pl.ds(pl.multiple_of(j * width, width), width)
            want = dot(member, goal[:, cols], 1, 0)
            resid = ((times * pred - want) * scale).astype(BF16)
            grad = dot(hidden, resid, 1, 0)
            total = grad if c == 0 else g2[j] + grad
            if c < chunks - 1:
                g2[j] = total
            else:
                g2b[j] = total.astype(BF16)
            dh = dot(f2[j], resid, 1, 1)
            dz = (dh * slope).astype(BF16)
            if fold == 1:
                dzbuf[j] = dz
            else:
                flat = dot(fold_matrix(fold), dz, 1, 0)
                folded = flat[:tall]
                for q in range(1, fold):
                    folded = folded + pltpu.roll(flat[q * tall:(q + 1) * tall], q * span, 1)
                dzbuf[j, pl.ds(0, tall), :] = folded.astype(BF16)
            return carry

        lax.fori_loop(0, lb, middle, 0)

        def back(g, carry):
            rows_in = dzbuf[:, pl.ds(pl.multiple_of(g * part, part), part), :].reshape(width, CH)
            out = dot(perm, rows_in, 0, 0).astype(BF16)
            bsend[c, pl.ds(g * many, many), cells(c)] = out.reshape(many, cell // fold, CH)
            return carry

        lax.fori_loop(0, n // many, back, 0)
        keep_own(second, c, cells(c))
        waiting = (second, c)

    feed(waiting, 0, 1)

    out2 = pltpu.make_async_copy(g2b, g2_hbm, out_sem.at[0])
    out2.start()

    for c in range(chunks):
        fold = folds[c]
        few = lb // fold
        await_all(brecv, brecv_sem, c)

        def last(p, carry):
            at = pl.ds(pl.multiple_of(p * 2 * lb, 2 * lb), 2 * lb)
            both = brecv[c, :, at, :].astype(F32)
            for h in range(2):
                d = both[:, h * lb:(h + 1) * lb, :].reshape(width, CH).astype(BF16)
                for q in range(fold):
                    i = q * few + p * 2 + h
                    grad = dot(xt[c, i], d, 1, 1)
                    total = grad if c == 0 else g1[i] + grad
                    if c < chunks - 1:
                        g1[i] = total
                    else:
                        g1b[i] = total.astype(BF16)
            return carry

        lax.fori_loop(0, few // 2, last, 0)

    out1 = pltpu.make_async_copy(g1b, g1_hbm, out_sem.at[1])
    out1.start()
    for c in range(chunks):
        await_all(send, send_sem, c)
        await_all(bsend, bsend_sem, c)
    out2.wait()
    out1.wait()


def fused(n, scale, which, folds, picks, place, archive, first_factor, second_factor, targets):
    rows = targets.shape[0]
    lb, width, _ = first_factor.shape
    chunks = len(folds)
    any_ = pl.BlockSpec(memory_space=pl.ANY)
    grads = jax.ShapeDtypeStruct((lb, width, width), BF16)
    block = pltpu.VMEM((chunks, n, lb * lb, CH), BF16)
    dma = pltpu.SemaphoreType.DMA
    return pl.pallas_call(
        functools.partial(kernel, n, lb, folds, scale),
        out_shape=(grads, grads),
        in_specs=[pl.BlockSpec(memory_space=pltpu.VMEM)] * 2 + [any_] * 4,
        out_specs=(any_, any_),
        scratch_shapes=[
            pltpu.VMEM(archive.shape, BF16),
            pltpu.VMEM(first_factor.shape, BF16),
            pltpu.VMEM(second_factor.shape, BF16),
            pltpu.VMEM(targets.shape, BF16),
            pltpu.VMEM(first_factor.shape, BF16),
            pltpu.VMEM((lb, CH, width), BF16),
            pltpu.VMEM((chunks, lb, width, CH), BF16),
            block, block, block, block,
            pltpu.VMEM((lb, width, CH), F32),
            pltpu.VMEM((lb, width, CH), BF16),
            pltpu.VMEM((lb, width, width), F32),
            pltpu.VMEM((lb, width, width), F32),
            pltpu.VMEM(first_factor.shape, BF16),
            pltpu.VMEM(first_factor.shape, BF16),
            pltpu.VMEM((rows, archive.shape[0]), BF16),
            pltpu.VMEM((max(folds), CH, archive.shape[0]), BF16),
            dma((2,)), dma((lb // 2,)), dma((lb // 2,)), dma((2,)),
            dma((chunks,)), dma((chunks,)), dma((chunks,)), dma((chunks,)),
        ],
        compiler_params=pltpu.CompilerParams(
            collective_id=which, has_side_effects=True, vmem_limit_bytes=60 * 1024 * 1024),
        cost_estimate=pl.CostEstimate(flops=10 * rows * lb * width * width, bytes_accessed=16 * 2**20, transcendentals=0),
    )(picks, place, archive, first_factor, second_factor, targets)


def widener(one, two, wide_one, wide_two):
    wide_one[...] = one[...].astype(F32)
    wide_two[...] = two[...].astype(F32)


def widen(one, two):
    lb, width, _ = one.shape
    spec = pl.BlockSpec((2, width, width), lambda i: (i, 0, 0))
    wide = jax.ShapeDtypeStruct(one.shape, F32)
    return pl.pallas_call(
        widener, grid=(lb // 2,), out_shape=(wide, wide), in_specs=[spec, spec], out_specs=(spec, spec),
    )(one, two)


def distinct(n, scale, archive, picks, first_factor, second_factor, targets):
    chunks = picks.shape[0] // CH
    picks = picks.reshape(chunks, CH)
    place, count = rank(picks, archive.shape[0])
    count = count[0, 0]
    if lax.axis_size("grp") * lax.axis_size("dp") > 1:
        count = lax.pmax(count, ("grp", "dp"))
    plans = [(1,) * (chunks - 1) + (fold,) for fold in FOLDS]
    index = 0
    for folds in plans[:-1]:
        index = index + (count > sum(CH // fold for fold in folds)).astype(jnp.int32)
    calls = [functools.partial(fused, n, scale, which, folds) for which, folds in enumerate(plans)]
    one, two = lax.switch(index, calls, picks, place, archive, first_factor, second_factor, targets)
    return widen(one, two)


def plain(archive, picks, first_factor, second_factor, targets, scale):
    rows = picks.shape[0]
    local_blocks = first_factor.shape[0]
    width = first_factor.shape[1]
    x = jnp.take(archive, picks, axis=0).reshape(rows, local_blocks, width)
    y_first = jnp.einsum("sia,iab->ibs", x, first_factor, preferred_element_type=F32).astype(BF16)
    z = lax.all_to_all(y_first, "feat", split_axis=1, concat_axis=0, tiled=True)
    z_float = z.astype(F32)
    hidden = jax.nn.gelu(z_float).astype(BF16)
    pred = jnp.einsum("ijs,jik->sjk", hidden, second_factor, preferred_element_type=F32)
    goal = targets.reshape(rows, local_blocks, width).astype(F32)
    resid = ((pred - goal) * scale).astype(BF16)
    grad_two = jnp.einsum("ijs,sjk->jik", hidden, resid, preferred_element_type=F32)
    d_hidden = jnp.einsum("sjk,jik->ijs", resid, second_factor, preferred_element_type=F32)
    d_z = jax.vjp(jax.nn.gelu, z_float)[1](d_hidden)[0].astype(BF16)
    d_first = lax.all_to_all(d_z, "feat", split_axis=0, concat_axis=1, tiled=True)
    grad_one = jnp.einsum("sia,ibs->iab", x, d_first, preferred_element_type=F32)
    return grad_one, grad_two


def local(archive, picks, first_factor, second_factor, targets):
    rows = picks.shape[0]
    lb, width, _ = first_factor.shape
    n = lax.axis_size("feat")
    dp = lax.axis_size("dp")
    scale = 1.0 / math.sqrt(rows * dp)
    args = (archive, picks, first_factor, second_factor, targets)
    fits = (lb == 8 and n * lb == width and width == 256 and n == 32 and rows % CH == 0
            and archive.shape[0] % CH == 0 and archive.shape[0] <= 1024 and rows <= 512)
    if fits:
        grad_one, grad_two = distinct(n, scale, *args)
    else:
        grad_one, grad_two = plain(*args, scale)
    if dp > 1:
        half = width // dp
        offset = lax.axis_index("dp") * half
        one, two = lax.psum((grad_one.astype(BF16), grad_two.astype(BF16)), "dp")
        grad_one = lax.dynamic_slice_in_dim(one.astype(F32), offset, half, 1)
        grad_two = lax.dynamic_slice_in_dim(two.astype(F32), offset, half, 1)
    return grad_one, grad_two


def solution(mesh):
    return jax.shard_map(
        local,
        mesh=mesh,
        in_specs=(
            P("grp", "feat"),
            P(("grp", "dp")),
            P(("grp", "feat"), None, None),
            P(("grp", "feat"), None, None),
            P(("grp", "dp"), "feat"),
        ),
        out_specs=(P(("grp", "feat"), "dp", None), P(("grp", "feat"), "dp", None)),
        check_vma=False,
    )
```

```python
import functools
import math

import jax
import jax.numpy as jnp
from jax import lax
from jax.experimental import pallas as pl
from jax.experimental.pallas import tpu as pltpu
from jax.sharding import PartitionSpec as P

BF16 = jnp.bfloat16
F32 = jnp.float32
CH = 128
FOLDS = (4, 1)
ROOT = math.sqrt(2.0 / math.pi)
CUBE = 0.044715


def dot(a, b, ca, cb):
    return lax.dot_general(a, b, (((ca,), (cb,)), ((), ())), preferred_element_type=F32)


def flip(me, k, n):
    out = 0
    bit = 1
    while bit < n:
        out = out + ((me // bit + k // bit) % 2) * bit
        bit *= 2
    return out


def ranker(picks, place, count):
    chunks = picks.shape[0]
    blocks = place.shape[0]
    lane = lax.broadcasted_iota(jnp.int32, (CH, CH), 1)
    sub = lax.broadcasted_iota(jnp.int32, (CH, CH), 0)
    hits = [jnp.zeros((8, CH), F32) for _ in range(blocks)]
    for c in range(chunks):
        col = jnp.broadcast_to(picks[pl.ds(c, 1), :].astype(F32), (CH, CH)).T.astype(jnp.int32)
        for b in range(blocks):
            hit = (col == lane + b * CH).astype(F32)
            hits[b] = jnp.maximum(hits[b], jnp.max(hit.reshape(CH // 8, 8, CH), axis=0))
    seen = jnp.concatenate([jnp.max(h, axis=0, keepdims=True) for h in hits], axis=0)
    seen_b = seen.astype(BF16)
    before = dot(seen_b, (sub < lane).astype(BF16), 1, 0)
    rows = lax.broadcasted_iota(jnp.int32, (blocks, blocks), 0)
    cols = lax.broadcasted_iota(jnp.int32, (blocks, blocks), 1)
    above = jnp.sum(dot((cols < rows).astype(BF16), seen_b, 1, 0), axis=1, keepdims=True)
    place[...] = jnp.where(seen > 0.5, before + above, -1.0).astype(jnp.int32)
    count[0, 0] = jnp.sum(seen).astype(jnp.int32)


def rank(picks, patterns):
    return pl.pallas_call(
        ranker,
        out_shape=(jax.ShapeDtypeStruct((patterns // CH, CH), jnp.int32), jax.ShapeDtypeStruct((1, 1), jnp.int32)),
        in_specs=[pl.BlockSpec(memory_space=pltpu.VMEM)],
        out_specs=(pl.BlockSpec(memory_space=pltpu.VMEM), pl.BlockSpec(memory_space=pltpu.SMEM)),
    )(picks)


def kernel(n, lb, folds, scale, picks, place, arch_hbm, f1_hbm, f2_hbm, goal_hbm, g1_hbm, g2_hbm,
           arch, f1, f2, goal, f1t, xc, xt, send, recv, bsend, brecv, zbuf, dzbuf, g1, g2, g1b, g2b, hot, pick_keep,
           in_sem, f1_sem, arch_sem, out_sem, send_sem, recv_sem, bsend_sem, brecv_sem):
    me = lax.axis_index("feat")
    width = n * lb
    rows = goal.shape[0]
    chunks = len(folds)
    patterns = arch.shape[0]
    blocks = patterns // CH
    cell = lb * lb
    per = width // cell
    part = per * lb

    def load_pair(p):
        some = pl.ds(p * 2, 2)
        cols = pl.ds(pl.multiple_of(p * 2 * width, 2 * width), 2 * width)
        return (pltpu.make_async_copy(f1_hbm.at[some], f1.at[some], f1_sem.at[p]),
                pltpu.make_async_copy(arch_hbm.at[:, cols], arch.at[:, cols], arch_sem.at[p]))

    loads = [
        pltpu.make_async_copy(src, dst, in_sem.at[t])
        for t, (src, dst) in enumerate(((f2_hbm, f2), (goal_hbm, goal)))
    ]
    for p in range(lb // 2):
        for load in load_pair(p):
            load.start()
    for load in loads:
        load.start()

    barrier = pltpu.get_barrier_semaphore()

    def greet(k, carry):
        pl.semaphore_signal(barrier, inc=1, device_id={"feat": flip(me, k, n)}, device_id_type=pl.DeviceIdType.MESH)
        return carry

    lax.fori_loop(1, n, greet, 0)

    left = lax.broadcasted_iota(jnp.int32, (width, width), 0)
    right = lax.broadcasted_iota(jnp.int32, (width, width), 1)
    perm = ((right % lb) * part + right // lb == left).astype(BF16)

    def fold_matrix(fold):
        few = lb // fold
        i = right % lb
        return ((i // few) * (n * few) + (right // lb) * few + i % few == left).astype(BF16)

    def chosen(c, q):
        span = CH // folds[c]
        row = lax.broadcasted_iota(jnp.int32, (CH, CH), 0) - q * span
        slot = jnp.where((row >= 0) & (row < span), row + c * CH, -2)
        return jnp.concatenate(
            [(place[pl.ds(b, 1), :] == slot).astype(BF16) for b in range(blocks)], axis=1)

    def cells(c):
        return pl.ds(0, cell // folds[c])

    def copy_to(sbuf, rbuf, ssem, rsem, c, peer, at):
        return pltpu.make_async_remote_copy(
            src_ref=sbuf.at[c, peer, at], dst_ref=rbuf.at[c, me, at],
            send_sem=ssem.at[c], recv_sem=rsem.at[c],
            device_id={"feat": peer}, device_id_type=pl.DeviceIdType.MESH)

    def send_all(sbuf, rbuf, ssem, rsem, c, at):
        def one(t, carry):
            peer = flip(me, n - 1 - t, n)
            copy_to(sbuf, rbuf, ssem, rsem, c, peer, at).start()
            return carry

        lax.fori_loop(0, n - 1, one, 0)
        rbuf[c, me, at] = sbuf[c, me, at]

    def await_all(buf, sem, c):
        block = buf.at[c, pl.ds(0, n - 1), cells(c)]
        pltpu.make_async_copy(block, block, sem.at[c]).wait()

    for c in range(chunks):
        fold = folds[c]
        few = lb // fold
        for q in range(fold):
            pick_keep[q] = chosen(c, q)

        def forward(p, carry):
            both = []
            if c == 0:
                for load in load_pair(p):
                    load.wait()
                for h in range(2):
                    f1t[p * 2 + h] = f1[p * 2 + h].T
            for h in range(2):
                y = None
                for q in range(fold):
                    i = q * few + p * 2 + h
                    cols = pl.ds(pl.multiple_of(i * width, width), width)
                    x = dot(pick_keep[q], arch[:, cols], 1, 0).astype(BF16)
                    xc[i] = x
                    term = dot(f1t[i], x, 1, 1)
                    y = term if y is None else y + term
                both.append(y.reshape(n, lb, CH))
            at = pl.ds(pl.multiple_of(p * 2 * lb, 2 * lb), 2 * lb)
            send[c, :, at, :] = jnp.concatenate(both, axis=1).astype(BF16)
            if c == 0:
                send_all(send, recv, send_sem, recv_sem, c, at)
            return carry

        if c == 0:
            pl.semaphore_wait(barrier, n - 1)
        lax.fori_loop(0, few // 2, forward, 0)
        if c > 0:
            send_all(send, recv, send_sem, recv_sem, c, cells(c))

        def turn_x(i, carry):
            xt[c, i] = xc[i].T
            return carry

        lax.fori_loop(0, lb, turn_x, 0)

    for c in range(rows // CH):
        col = jnp.broadcast_to(picks[pl.ds(c, 1), :].astype(F32), (CH, CH)).T.astype(jnp.int32)
        lane = lax.broadcasted_iota(jnp.int32, (CH, CH), 1)
        for b in range(blocks):
            hot[c * CH:(c + 1) * CH, b * CH:(b + 1) * CH] = (col == lane + b * CH).astype(BF16)

    loads[0].wait()
    loads[1].wait()

    for c in range(chunks):
        fold = folds[c]
        span = CH // fold
        tall = width // fold
        member = dot(chosen(c, 0), hot[...], 1, 1)
        times = jnp.sum(member, axis=1, keepdims=True)
        member = member.astype(BF16)
        many = per * fold
        await_all(recv, recv_sem, c)

        def permute(g, carry):
            got = recv[c, pl.ds(g * many, many), cells(c)].reshape(width, CH)
            z = dot(perm, got, 1, 0).reshape(lb, part, CH)
            zbuf[:, pl.ds(pl.multiple_of(g * part, part), part), :] = z
            return carry

        lax.fori_loop(0, n // many, permute, 0)

        def middle(j, carry):
            if fold == 1:
                z = zbuf[j]
            else:
                flat = zbuf[j, pl.ds(0, tall), :]
                pieces = [flat if q == 0 else pltpu.roll(flat, CH - q * span, 1) for q in range(fold)]
                z = dot(fold_matrix(fold), jnp.concatenate(pieces, axis=0).astype(BF16), 0, 0)
            sq = z * z
            t = jnp.tanh(ROOT * z * (1.0 + CUBE * sq))
            half = 0.5 * (1.0 + t)
            hidden = (z * half).astype(BF16)
            slope = half + 0.5 * z * (1.0 - t * t) * (ROOT * (1.0 + 3.0 * CUBE * sq))
            pred = dot(hidden, f2[j], 0, 0)
            cols = pl.ds(pl.multiple_of(j * width, width), width)
            want = dot(member, goal[:, cols], 1, 0)
            resid = ((times * pred - want) * scale).astype(BF16)
            grad = dot(hidden, resid, 1, 0)
            total = grad if c == 0 else g2[j] + grad
            if c < chunks - 1:
                g2[j] = total
            else:
                g2b[j] = total.astype(BF16)
            dh = dot(f2[j], resid, 1, 1)
            dz = (dh * slope).astype(BF16)
            if fold == 1:
                dzbuf[j] = dz
            else:
                flat = dot(fold_matrix(fold), dz, 1, 0)
                folded = flat[:tall]
                for q in range(1, fold):
                    folded = folded + pltpu.roll(flat[q * tall:(q + 1) * tall], q * span, 1)
                dzbuf[j, pl.ds(0, tall), :] = folded.astype(BF16)
            return carry

        lax.fori_loop(0, lb, middle, 0)

        def back(g, carry):
            rows_in = dzbuf[:, pl.ds(pl.multiple_of(g * part, part), part), :].reshape(width, CH)
            out = dot(perm, rows_in, 0, 0).astype(BF16)
            bsend[c, pl.ds(g * many, many), cells(c)] = out.reshape(many, cell // fold, CH)
            return carry

        lax.fori_loop(0, n // many, back, 0)
        send_all(bsend, brecv, bsend_sem, brecv_sem, c, cells(c))

    out2 = pltpu.make_async_copy(g2b, g2_hbm, out_sem.at[0])
    out2.start()

    for c in range(chunks):
        fold = folds[c]
        few = lb // fold
        await_all(brecv, brecv_sem, c)

        def last(p, carry):
            at = pl.ds(pl.multiple_of(p * 2 * lb, 2 * lb), 2 * lb)
            both = brecv[c, :, at, :].astype(F32)
            for h in range(2):
                d = both[:, h * lb:(h + 1) * lb, :].reshape(width, CH).astype(BF16)
                for q in range(fold):
                    i = q * few + p * 2 + h
                    grad = dot(xt[c, i], d, 1, 1)
                    total = grad if c == 0 else g1[i] + grad
                    if c < chunks - 1:
                        g1[i] = total
                    else:
                        g1b[i] = total.astype(BF16)
            return carry

        lax.fori_loop(0, few // 2, last, 0)

    out1 = pltpu.make_async_copy(g1b, g1_hbm, out_sem.at[1])
    out1.start()
    for c in range(chunks):
        await_all(send, send_sem, c)
        await_all(bsend, bsend_sem, c)
    out2.wait()
    out1.wait()


def fused(n, scale, which, folds, picks, place, archive, first_factor, second_factor, targets):
    rows = targets.shape[0]
    lb, width, _ = first_factor.shape
    chunks = len(folds)
    any_ = pl.BlockSpec(memory_space=pl.ANY)
    grads = jax.ShapeDtypeStruct((lb, width, width), BF16)
    block = pltpu.VMEM((chunks, n, lb * lb, CH), BF16)
    dma = pltpu.SemaphoreType.DMA
    return pl.pallas_call(
        functools.partial(kernel, n, lb, folds, scale),
        out_shape=(grads, grads),
        in_specs=[pl.BlockSpec(memory_space=pltpu.VMEM)] * 2 + [any_] * 4,
        out_specs=(any_, any_),
        scratch_shapes=[
            pltpu.VMEM(archive.shape, BF16),
            pltpu.VMEM(first_factor.shape, BF16),
            pltpu.VMEM(second_factor.shape, BF16),
            pltpu.VMEM(targets.shape, BF16),
            pltpu.VMEM(first_factor.shape, BF16),
            pltpu.VMEM((lb, CH, width), BF16),
            pltpu.VMEM((chunks, lb, width, CH), BF16),
            block, block, block, block,
            pltpu.VMEM((lb, width, CH), F32),
            pltpu.VMEM((lb, width, CH), BF16),
            pltpu.VMEM((lb, width, width), F32),
            pltpu.VMEM((lb, width, width), F32),
            pltpu.VMEM(first_factor.shape, BF16),
            pltpu.VMEM(first_factor.shape, BF16),
            pltpu.VMEM((rows, archive.shape[0]), BF16),
            pltpu.VMEM((max(folds), CH, archive.shape[0]), BF16),
            dma((2,)), dma((lb // 2,)), dma((lb // 2,)), dma((2,)),
            dma((chunks,)), dma((chunks,)), dma((chunks,)), dma((chunks,)),
        ],
        compiler_params=pltpu.CompilerParams(
            collective_id=which, has_side_effects=True, vmem_limit_bytes=60 * 1024 * 1024),
        cost_estimate=pl.CostEstimate(flops=10 * rows * lb * width * width, bytes_accessed=16 * 2**20, transcendentals=0),
    )(picks, place, archive, first_factor, second_factor, targets)


def widener(one, two, wide_one, wide_two):
    wide_one[...] = one[...].astype(F32)
    wide_two[...] = two[...].astype(F32)


def widen(one, two):
    lb, width, _ = one.shape
    spec = pl.BlockSpec((2, width, width), lambda i: (i, 0, 0))
    wide = jax.ShapeDtypeStruct(one.shape, F32)
    return pl.pallas_call(
        widener, grid=(lb // 2,), out_shape=(wide, wide), in_specs=[spec, spec], out_specs=(spec, spec),
    )(one, two)


def distinct(n, scale, archive, picks, first_factor, second_factor, targets):
    chunks = picks.shape[0] // CH
    picks = picks.reshape(chunks, CH)
    place, count = rank(picks, archive.shape[0])
    count = count[0, 0]
    if lax.axis_size("grp") * lax.axis_size("dp") > 1:
        count = lax.pmax(count, ("grp", "dp"))
    plans = [(1,) * (chunks - 1) + (fold,) for fold in FOLDS]
    index = 0
    for folds in plans[:-1]:
        index = index + (count > sum(CH // fold for fold in folds)).astype(jnp.int32)
    calls = [functools.partial(fused, n, scale, which, folds) for which, folds in enumerate(plans)]
    one, two = lax.switch(index, calls, picks, place, archive, first_factor, second_factor, targets)
    return widen(one, two)


def plain(archive, picks, first_factor, second_factor, targets, scale):
    rows = picks.shape[0]
    local_blocks = first_factor.shape[0]
    width = first_factor.shape[1]
    x = jnp.take(archive, picks, axis=0).reshape(rows, local_blocks, width)
    y_first = jnp.einsum("sia,iab->ibs", x, first_factor, preferred_element_type=F32).astype(BF16)
    z = lax.all_to_all(y_first, "feat", split_axis=1, concat_axis=0, tiled=True)
    z_float = z.astype(F32)
    hidden = jax.nn.gelu(z_float).astype(BF16)
    pred = jnp.einsum("ijs,jik->sjk", hidden, second_factor, preferred_element_type=F32)
    goal = targets.reshape(rows, local_blocks, width).astype(F32)
    resid = ((pred - goal) * scale).astype(BF16)
    grad_two = jnp.einsum("ijs,sjk->jik", hidden, resid, preferred_element_type=F32)
    d_hidden = jnp.einsum("sjk,jik->ijs", resid, second_factor, preferred_element_type=F32)
    d_z = jax.vjp(jax.nn.gelu, z_float)[1](d_hidden)[0].astype(BF16)
    d_first = lax.all_to_all(d_z, "feat", split_axis=0, concat_axis=1, tiled=True)
    grad_one = jnp.einsum("sia,ibs->iab", x, d_first, preferred_element_type=F32)
    return grad_one, grad_two


def local(archive, picks, first_factor, second_factor, targets):
    rows = picks.shape[0]
    lb, width, _ = first_factor.shape
    n = lax.axis_size("feat")
    dp = lax.axis_size("dp")
    scale = 1.0 / math.sqrt(rows * dp)
    args = (archive, picks, first_factor, second_factor, targets)
    fits = (lb == 8 and n * lb == width and width == 256 and n == 32 and rows % CH == 0
            and archive.shape[0] % CH == 0 and archive.shape[0] <= 1024 and rows <= 512)
    if fits:
        grad_one, grad_two = distinct(n, scale, *args)
    else:
        grad_one, grad_two = plain(*args, scale)
    if dp > 1:
        half = width // dp
        offset = lax.axis_index("dp") * half
        one, two = lax.psum((grad_one.astype(BF16), grad_two.astype(BF16)), "dp")
        grad_one = lax.dynamic_slice_in_dim(one.astype(F32), offset, half, 1)
        grad_two = lax.dynamic_slice_in_dim(two.astype(F32), offset, half, 1)
    return grad_one, grad_two


def solution(mesh):
    return jax.shard_map(
        local,
        mesh=mesh,
        in_specs=(
            P("grp", "feat"),
            P(("grp", "dp")),
            P(("grp", "feat"), None, None),
            P(("grp", "feat"), None, None),
            P(("grp", "dp"), "feat"),
        ),
        out_specs=(P(("grp", "feat"), "dp", None), P(("grp", "feat"), "dp", None)),
        check_vma=False,
    )
```
